128 devices in a mesh: oi: 4 (over x), oj: 4 (over y_hi, core), vert: 8 (over y_lo, z).
Axes of the slice: x: 4, y: 4 (y_hi: 2, y_lo: 2; y = y_hi * 2 + y_lo), z: 4, core: 2. Of those that a mesh axis runs over, the one named last changes fastest.
Arguments:
- amps: bfloat16 [8192, 32768], P('oi', ('oj', 'vert')), may hold values from -6 to 6
- integrals: bfloat16 [32768, 4096], P(('oj', 'vert'), 'oi'), may hold values from -0.0625 to 0.0625
- amp_live: int32 [64, 256], P('oi', ('oj', 'vert')), may hold values 0 or 1
- int_live: int32 [256, 32], P(('oj', 'vert'), 'oi'), may hold values 0 or 1
- row_gap: float32 [8192], P('oi'), may hold values from 0.5 to 5
- col_gap: float32 [4096], P(('oj', 'vert')), may hold values from 0.5 to 5
Outputs:
- update: float32 [8192, 4096], P('oi', ('oj', 'vert'))
The draws below stay inside these ranges and needn't reach their ends.
All inputs are finite; a program needn't handle non-finite values. No bound on the sum of `amp_live` or of `int_live` on one device may be relied on, other than what follows from the above.
Results may differ from the reference program's by a relative error of at most 0.0003.
Values may be sent and summed in bfloat16 or wider, within the bound.
No kernel may reach another device: no remote copies, remote signals or barrier semaphores. Data moves between devices by JAX's collectives and lax.ppermute only.
A program may use at most 128 MiB of HBM per device.

```python
import math
import jax
import jax.numpy as jnp

VIRT_BLOCK = 128
ROWS = 8192
KDIM = 32768
COLS = 4096


def plant(array, stream_key, least, top_value):
    longest = array.shape.index(max(array.shape))
    spots = []
    for shift in (0, 1):
        where = [jax.random.randint(jax.random.fold_in(stream_key, axis), (), 0, length) for axis, length in enumerate(array.shape)]
        where[longest] = (where[longest] + shift) % array.shape[longest]
        spots.append(tuple(where))
    return array.at[spots[0]].set(least).at[spots[1]].set(top_value)


def raised(array, rng, source, target, blocks, factor):
    def block_of(axis_at):
        return (jnp.arange(array.shape[axis_at]) // (array.shape[axis_at] // blocks)).reshape((-1,) + (1,) * (array.ndim - 1 - axis_at))

    near = jax.random.permutation(rng, blocks)[block_of(target)]
    other_side = (block_of(target) + blocks // 2) % blocks
    return jnp.where((block_of(source) == near) | (block_of(source) == other_side), factor * array, array)


def level_of(stream_key, dims, pieces, smallest, largest):
    loudness, own = 1.0, jax.random.fold_in(stream_key, 6)
    for axis_at, parts in pieces:
        steps = jnp.exp(jax.random.uniform(jax.random.fold_in(own, axis_at), (parts,), jnp.float32, smallest / len(pieces), largest / len(pieces)))
        loudness = loudness * jnp.repeat(steps, dims[axis_at] // parts).reshape([-1 if axis == axis_at else 1 for axis in range(len(dims))])
    return loudness


def normal_values(rng, shape, deviation, reach, shards=(), kind=jnp.bfloat16):
    entries = jax.random.normal(rng, shape, jnp.float32) * deviation
    if len(shards) > 0:
        entries = level_of(rng, shape, shards, -0.22, 0.18) * entries
    return jnp.clip(entries, min=-reach, max=reach).astype(kind)


def bell_draw_with(key, dims, scale, bound, cuts, heavy, held_as=jnp.bfloat16):
    entries = scale * jax.random.normal(key, dims, jnp.float32)
    if cuts:
        entries = entries * level_of(key, dims, cuts, -0.22, 0.18)
    return jnp.clip(raised(entries, jax.random.fold_in(key, 3), *heavy), -bound, bound).astype(held_as)


def setup_inputs(seed: int = 0) -> dict:
    seeds = jax.random.split(jax.random.key(seed), 7)
    return {
        "amps": normal_values(seeds[0], (ROWS, KDIM), 1.0, 6.0, ((0, 4), (1, 32))),
        "integrals": bell_draw_with(seeds[1], (KDIM, COLS), KDIM ** -0.5, 0.0625, ((0, 32), (1, 4)), (0, 1, 32, 2.75)),
        "amp_live": plant((jax.random.randint(seeds[2], (ROWS // VIRT_BLOCK, KDIM // VIRT_BLOCK), 0, 5) < 3).astype(jnp.int32), jax.random.fold_in(seeds[2], 1), 0, 1),
        "int_live": plant((jax.random.randint(seeds[3], (KDIM // VIRT_BLOCK, COLS // VIRT_BLOCK), 0, 5) < 3).astype(jnp.int32), jax.random.fold_in(seeds[3], 1), 0, 1),
        "row_gap": jnp.clip(jnp.exp(math.log(5.0) - 2.3025851 * jax.random.uniform(seeds[4], (ROWS,), jnp.float32) ** level_of(seeds[4], (ROWS,), ((0, 4),), -0.2, 0.2)), 0.5, 5.0),
        "col_gap": jnp.clip(jnp.exp(math.log(5.0) - 2.3025851 * jax.random.uniform(seeds[5], (COLS,), jnp.float32) ** level_of(seeds[5], (COLS,), ((0, 32),), -0.2, 0.2)), 0.5, 5.0),
    }


def mask_tiles(values, live):
    tile_rows, tile_cols = live.shape
    block = values.shape[0] // tile_rows
    shaped = values.reshape(tile_rows, block, tile_cols, values.shape[1] // tile_cols)
    kept = shaped * live.astype(values.dtype)[:, None, :, None]
    return kept.reshape(values.shape)


def reference(amps, integrals, amp_live, int_live, row_gap, col_gap):
    amp_tiles = mask_tiles(amps, amp_live)
    int_tiles = mask_tiles(integrals, int_live)
    resid = jnp.dot(amp_tiles, int_tiles, preferred_element_type=jnp.float32)
    return resid / (row_gap[:, None] + col_gap[None, :])
```

```python
import functools
import jax
import jax.numpy as jnp
from jax import lax
from jax.experimental import pallas as pl
from jax.experimental.pallas import tpu as pltpu
from jax.sharding import PartitionSpec as P

AXES = ("oi", "oj", "vert")
SIDE = 4
LANES = 128
LANE_TILE = 512
TOP = 32512.0
STEPS_PER_OCTAVE = 64.0
VMEM_BYTES = 40 * 1024 * 1024


def place_of(i):
    x, rest = divmod(i, 32)
    y_hi, rest = divmod(rest, 16)
    core, rest = divmod(rest, 8)
    y_lo, z = divmod(rest, 4)
    return x, 2 * y_hi + y_lo, z, core


def index_in_plane(y, z, core):
    y, z = y % SIDE, z % SIDE
    return (((y // 2) * 2 + core) * 2 + y % 2) * 4 + z


def shift(value, dx=0, dy=0, dz=0, dcore=0):
    pairs = []
    for i in range(128):
        x, y, z, core = place_of(i)
        pairs.append((i, (x + dx) % SIDE * 32 + index_in_plane(y + dy, z + dz, (core + dcore) % 2)))
    return lax.ppermute(value, AXES, pairs)


def mask_tiles(values, live):
    tile_rows, tile_cols = live.shape
    block = values.shape[0] // tile_rows
    shaped = values.reshape(tile_rows, block, tile_cols, values.shape[1] // tile_cols)
    kept = shaped * live.astype(values.dtype)[:, None, :, None]
    return kept.reshape(values.shape)


def lane_index(rows):
    return lax.broadcasted_iota(jnp.int32, (rows, LANES), 1)


def store_codes(out, rows, lanes_at, tile, values):
    peak = jnp.maximum(jnp.max(jnp.abs(values), axis=1, keepdims=True), 1e-30)
    code = jnp.ceil(jnp.log2(peak) * STEPS_PER_OCTAVE)
    steps = jnp.round(values * (jnp.exp2(code * (-1.0 / STEPS_PER_OCTAVE)) * TOP))
    out[rows, pl.ds(lanes_at, LANE_TILE)] = steps.astype(jnp.int32).astype(jnp.int16)
    return code


def load_codes(ref, rows, tile):
    heads = ref[rows, pl.ds(ref.shape[1] - LANES, LANES)].astype(jnp.int32)
    code = jnp.sum(jnp.where(lane_index(heads.shape[0]) == tile, heads, 0), axis=1, keepdims=True)
    scale = jnp.exp2(code.astype(jnp.float32) * (1.0 / STEPS_PER_OCTAVE)) * (1.0 / TOP)
    return ref[rows, pl.ds(tile * LANE_TILE, LANE_TILE)].astype(jnp.int32).astype(jnp.float32) * scale


def store_heads(out, rows, n_rows, codes):
    lane = lane_index(n_rows)
    heads = jnp.zeros((n_rows, LANES), jnp.int32)
    for tile, code in codes:
        heads = jnp.where(lane == tile, code.astype(jnp.int32), heads)
    out[rows, pl.ds(out.shape[1] - LANES, LANES)] = heads.astype(jnp.int16)


def rows_of(order, n, at):
    if order == "z":
        return [pl.ds(pl.multiple_of((q * 4 + at) * n, 16), n) for q in range(4)]
    return [pl.ds(pl.multiple_of(at * 4 * n, 16), 4 * n)]


def product_kernel(order, n, n_pieces, table, *refs):
    pieces, (a_own, a_other), rest = refs[:n_pieces], refs[n_pieces:n_pieces + 2], refs[n_pieces + 2:]
    acc, outs = rest[-1], rest[:-1]
    tile = pl.program_id(0)
    depth = a_own.shape[0]
    at = 0
    for piece in pieces:
        m = piece.shape[0]
        acc[pl.ds(at, m), :] = jnp.dot(
            piece[:, pl.ds(0, depth)], a_own[...], preferred_element_type=jnp.float32
        ) + jnp.dot(piece[:, pl.ds(depth, depth)], a_other[...], preferred_element_type=jnp.float32)
        at += m
    lanes_at = pl.multiple_of(tile * LANE_TILE, LANE_TILE)

    def coded(out, into, source):
        code = store_codes(out, into, lanes_at, tile, acc[source, :])
        size = into.size
        heads_at = (into, pl.ds(out.shape[1] - LANES, LANES))
        before = jnp.where(tile == 0, 0, out[heads_at].astype(jnp.int32))
        out[heads_at] = jnp.where(lane_index(size) == tile, code.astype(jnp.int32), before).astype(jnp.int16)

    if order == "all":
        for y in range(4):
            coded(outs[0], pl.ds(y * 4 * n, 4 * n), rows_of("y", n, table[y])[0])
        return
    for to, out in enumerate(outs):
        row = 0
        for source in rows_of(order, n, table[to]):
            into = pl.ds(row, source.size)
            if to == 0:
                out[into, pl.ds(lanes_at, LANE_TILE)] = acc[source, :]
            else:
                coded(out, into, source)
            row += source.size


def products(order, n, table, pieces, a_own, a_other):
    depth, rows = a_own.shape
    if order == "all":
        out_shape = [jax.ShapeDtypeStruct((16 * n, rows + LANES), jnp.int16)]
    else:
        out_shape = [jax.ShapeDtypeStruct((4 * n, rows), jnp.float32)] + [
            jax.ShapeDtypeStruct((4 * n, rows + LANES), jnp.int16)
        ] * 3
    whole = lambda shape: pl.BlockSpec(shape, lambda j, t: (0, 0))
    flops = 2 * 16 * n * 2 * depth * rows
    moved = 16 * n * 4 * depth + 4 * depth * rows + 10 * n * rows * 2
    return pl.pallas_call(
        functools.partial(product_kernel, order, n, len(pieces)),
        out_shape=out_shape,
        grid_spec=pltpu.PrefetchScalarGridSpec(
            num_scalar_prefetch=1,
            grid=(rows // LANE_TILE,),
            in_specs=[whole(p.shape) for p in pieces]
            + [pl.BlockSpec((depth, LANE_TILE), lambda j, t: (0, j))] * 2,
            out_specs=[whole(s.shape) for s in out_shape],
            scratch_shapes=[pltpu.VMEM((16 * n, LANE_TILE), jnp.float32)],
        ),
        compiler_params=pltpu.CompilerParams(vmem_limit_bytes=VMEM_BYTES),
        cost_estimate=pl.CostEstimate(flops=flops, bytes_accessed=moved, transcendentals=0),
    )(table, *pieces, a_own, a_other)


def join_kernel(n, table, kept, one, two, three, *outs_and_scratch):
    *outs, total = outs_and_scratch
    rows = kept.shape[0]
    tiles = kept.shape[1] // LANE_TILE
    everything = pl.ds(0, rows)
    codes = [[] for _ in outs]
    for tile in range(tiles):
        lanes = pl.ds(tile * LANE_TILE, LANE_TILE)
        total[...] = kept[:, lanes] + sum(load_codes(ref, everything, tile) for ref in (one, two, three))
        for to, out in enumerate(outs):
            source = total[pl.ds(pl.multiple_of(table[to] * n, 16), n), :]
            if to == 0:
                out[:, lanes] = source
            else:
                codes[to].append((tile, store_codes(out, pl.ds(0, n), tile * LANE_TILE, tile, source)))
    for to in range(1, len(outs)):
        store_heads(outs[to], pl.ds(0, n), n, codes[to])


def join(n, table, kept, arrived):
    rows = kept.shape[1]
    out_shape = [jax.ShapeDtypeStruct((n, rows), jnp.float32)] + [
        jax.ShapeDtypeStruct((n, rows + LANES), jnp.int16)
    ] * 3
    vmem = pl.BlockSpec(memory_space=pltpu.VMEM)
    return pl.pallas_call(
        functools.partial(join_kernel, n),
        out_shape=out_shape,
        in_specs=[pl.BlockSpec(memory_space=pltpu.SMEM)] + [vmem] * 4,
        out_specs=[vmem] * 4,
        scratch_shapes=[pltpu.VMEM((4 * n, LANE_TILE), jnp.float32)],
        compiler_params=pltpu.CompilerParams(vmem_limit_bytes=VMEM_BYTES),
        cost_estimate=pl.CostEstimate(flops=40 * n * rows, bytes_accessed=50 * n * rows, transcendentals=0),
    )(table, kept, *arrived)


def last_kernel(kept, one, two, three, out):
    everything = pl.ds(0, kept.shape[0])
    for tile in range(kept.shape[1] // LANE_TILE):
        lanes = pl.ds(tile * LANE_TILE, LANE_TILE)
        out[:, lanes] = kept[:, lanes] + sum(load_codes(ref, everything, tile) for ref in (one, two, three))


def last(kept, arrived):
    vmem = pl.BlockSpec(memory_space=pltpu.VMEM)
    return pl.pallas_call(
        last_kernel,
        out_shape=jax.ShapeDtypeStruct(kept.shape, jnp.float32),
        in_specs=[vmem] * 4,
        out_specs=vmem,
        compiler_params=pltpu.CompilerParams(vmem_limit_bytes=VMEM_BYTES),
        cost_estimate=pl.CostEstimate(flops=10 * kept.size, bytes_accessed=14 * kept.size, transcendentals=0),
    )(kept, *arrived)


def sum_kernel(n, arrived, out):
    for tile in range(out.shape[1] // LANE_TILE):
        out[:, pl.ds(tile * LANE_TILE, LANE_TILE)] = sum(
            load_codes(arrived, pl.ds(k * n, n), tile) for k in range(16)
        )


def sum_of(n, arrived):
    rows = arrived.shape[1] - LANES
    vmem = pl.BlockSpec(memory_space=pltpu.VMEM)
    return pl.pallas_call(
        functools.partial(sum_kernel, n),
        out_shape=jax.ShapeDtypeStruct((n, rows), jnp.float32),
        in_specs=[vmem],
        out_specs=vmem,
        compiler_params=pltpu.CompilerParams(vmem_limit_bytes=VMEM_BYTES),
        cost_estimate=pl.CostEstimate(flops=50 * n * rows, bytes_accessed=36 * n * rows, transcendentals=0),
    )(arrived)


PLANE_GROUPS = [[index_in_plane(y, z, core) for y in range(4) for z in range(4)] for core in range(2)]
CHUNKS = (32, 32)
ORDERS_NEAR = ("z", "y")
ORDERS_FAR = ("z", "all")


def per_device(amps, integrals, amp_live, int_live, row_gap, col_gap):
    x = lax.axis_index("oi")
    oj, vert = lax.axis_index("oj"), lax.axis_index("vert")
    core, y, z = oj % 2, (oj // 2) * 2 + vert // 4, vert % 4
    around = jnp.arange(4, dtype=jnp.int32)

    int_t = mask_tiles(integrals, int_live).T.reshape(8, 2, 64, integrals.shape[0])
    mine = lax.dynamic_index_in_dim(int_t, core, 1, keepdims=False)
    theirs = lax.dynamic_index_in_dim(int_t, 1 - core, 1, keepdims=False)
    both = jnp.concatenate([mine, shift(theirs, dcore=1)], axis=2)
    a_own = mask_tiles(amps, amp_live).T
    a_other = shift(a_own, dcore=1)

    def y_table(first_block, places):
        pair = jnp.where(places // 2 == (first_block % 4) // 2, 0, 1)
        return (pair * 2 + places % 2).astype(jnp.int32)

    def spread(order, n, first_block, pieces):
        if order == "all":
            (sent,) = products(order, n, y_table(first_block, around), pieces, a_own, a_other)
            got = lax.all_to_all(sent, ("oj", "vert"), 0, 0, axis_index_groups=PLANE_GROUPS, tiled=True)
            return sum_of(n, got)
        z_rel, y_rel = ((z + around) % 4).astype(jnp.int32), y_table(first_block, (y + around) % 4)
        along_z = [functools.partial(shift, dz=d) for d in (1, 2, 3)]
        along_y = [functools.partial(shift, dy=d) for d in (1, 2, 3)]
        steps = [(z_rel, along_z), (y_rel, along_y)]
        if order == "y":
            steps = steps[::-1]
        kept, *sent = products(order, n, steps[0][0], pieces, a_own, a_other)
        arrived = [go(s) for go, s in zip(steps[0][1], sent)]
        kept, *sent = join(n, steps[1][0], kept, arrived)
        return last(kept, [go(s) for go, s in zip(steps[1][1], sent)])

    near, far = [], []
    offset = 0
    own, left, right = [], [], []
    for n in CHUNKS:
        own.append(both[:, offset:offset + n].reshape(8 * n, both.shape[2]))
        offset += n
        left.append(shift(own[-1], dx=1))
        right.append(shift(own[-1], dx=-1))
    for j, n in enumerate(CHUNKS):
        near.append(spread(ORDERS_NEAR[j], n, x - 1, [left[j], right[j]]))
        low = shift(left[j][:4 * n], dx=1)
        high = shift(right[j][4 * n:], dx=-1)
        far.append(spread(ORDERS_FAR[j], n, x, [own[j], low, high]))
    near, far = jnp.concatenate(near), jnp.concatenate(far)
    far_is_mine = core == x % 2
    kept = jnp.where(far_is_mine, far, near)
    swapped = shift(jnp.where(far_is_mine, near, far), dcore=1)
    resid = jnp.where(core == 0, jnp.concatenate([kept, swapped]), jnp.concatenate([swapped, kept])).T
    return resid / (row_gap[:, None] + col_gap[None, :])


def solution(mesh):
    return jax.shard_map(
        per_device,
        mesh=mesh,
        in_specs=(
            P("oi", ("oj", "vert")),
            P(("oj", "vert"), "oi"),
            P("oi", ("oj", "vert")),
            P(("oj", "vert"), "oi"),
            P("oi"),
            P(("oj", "vert")),
        ),
        out_specs=P("oi", ("oj", "vert")),
        check_vma=False,
    )
```

```python
import functools
import jax
import jax.numpy as jnp
from jax import lax
from jax.experimental import pallas as pl
from jax.experimental.pallas import tpu as pltpu
from jax.sharding import PartitionSpec as P

AXES = ("oi", "oj", "vert")
SIDE = 4
LANES = 128
LANE_TILE = 512
TOP = 32512.0
STEPS_PER_OCTAVE = 64.0
VMEM_BYTES = 16 * 1024 * 1024


def place_of(i):
    x, rest = divmod(i, 32)
    y_hi, rest = divmod(rest, 16)
    core, rest = divmod(rest, 8)
    y_lo, z = divmod(rest, 4)
    return x, 2 * y_hi + y_lo, z, core


def index_in_plane(y, z, core):
    y, z = y % SIDE, z % SIDE
    return (((y // 2) * 2 + core) * 2 + y % 2) * 4 + z


def shift(value, dx=0, dcore=0, dplane=None):
    pairs = []
    for i in range(128):
        x, y, z, core = place_of(i)
        dy, dz = dplane[core] if dplane else (0, 0)
        pairs.append((i, (x + dx) % SIDE * 32 + index_in_plane(y + dy, z + dz, (core + dcore) % 2)))
    return lax.ppermute(value, AXES, pairs)


def after(value, *others):
    return lax.optimization_barrier((value, others))[0]


def lane_index(rows):
    return lax.broadcasted_iota(jnp.int32, (rows, LANES), 1)


def encode(values, steps, heads, tile):
    for at in range(0, values.shape[0], 32):
        rows = pl.ds(at, min(32, values.shape[0] - at))
        part = values[rows, :]
        peak = jnp.maximum(jnp.max(jnp.abs(part), axis=1, keepdims=True), 1e-30)
        code = jnp.ceil(jnp.log2(peak) * STEPS_PER_OCTAVE)
        scaled = jnp.round(part * (jnp.exp2(code * (-1.0 / STEPS_PER_OCTAVE)) * TOP))
        steps[rows, :] = scaled.astype(jnp.int32).astype(jnp.int16)
        heads[rows, :] = jnp.where(lane_index(rows.size) == tile, code.astype(jnp.int32), heads[rows, :])


def load_codes(ref, rows, tile):
    heads = ref[rows, pl.ds(ref.shape[1] - LANES, LANES)].astype(jnp.int32)
    code = jnp.sum(jnp.where(lane_index(heads.shape[0]) == tile, heads, 0), axis=1, keepdims=True)
    scale = jnp.exp2(code.astype(jnp.float32) * (1.0 / STEPS_PER_OCTAVE)) * (1.0 / TOP)
    return ref[rows, pl.ds(tile * LANE_TILE, LANE_TILE)].astype(jnp.int32).astype(jnp.float32) * scale


def params():
    return pltpu.CompilerParams(vmem_limit_bytes=VMEM_BYTES)


def cost(micros):
    return pl.CostEstimate(flops=int(micros * 1.15e9), bytes_accessed=1000, transcendentals=0)


def turned_kernel(core, live, values, mine, theirs, scratch):
    tile = pl.program_id(0)
    for k in range(values.shape[0] // LANES):
        part = values[pl.ds(k * LANES, LANES), :]
        kept = jnp.where(live[k, tile] != 0, part, jnp.zeros_like(part))
        scratch[:, pl.ds(k * LANES, LANES)] = kept.T
    mine[0] = scratch[pl.ds(pl.multiple_of(core[0] * 64, 16), 64), :]
    theirs[0] = scratch[pl.ds(pl.multiple_of((1 - core[0]) * 64, 16), 64), :]


def turned(core, values, live):
    depth, columns = values.shape
    half = jax.ShapeDtypeStruct((columns // LANES, 64, depth), jnp.bfloat16)
    smem = pl.BlockSpec(memory_space=pltpu.SMEM)
    return pl.pallas_call(
        turned_kernel,
        grid=(columns // LANES,),
        out_shape=[half, half],
        in_specs=[smem, smem, pl.BlockSpec((depth, LANES), lambda t: (0, t))],
        out_specs=[pl.BlockSpec((1, 64, depth), lambda t: (t, 0, 0))] * 2,
        scratch_shapes=[pltpu.VMEM((LANES, depth), jnp.bfloat16)],
        compiler_params=params(),
        cost_estimate=cost(2.5),
    )(core.reshape(1), live, values)


def amps_kernel(live, values, out):
    tile = pl.program_id(0)
    for r in range(values.shape[0] // LANES):
        for k in range(values.shape[1] // LANES):
            part = values[pl.ds(r * LANES, LANES), pl.ds(k * LANES, LANES)]
            kept = jnp.where(live[tile * (values.shape[0] // LANES) + r, k] != 0, part, jnp.zeros_like(part))
            out[pl.ds(k * LANES, LANES), pl.ds(r * LANES, LANES)] = kept.T


def turned_amps(values, live):
    rows, depth = values.shape
    return pl.pallas_call(
        amps_kernel,
        grid=(rows // LANE_TILE,),
        out_shape=jax.ShapeDtypeStruct((depth, rows), jnp.bfloat16),
        in_specs=[pl.BlockSpec(memory_space=pltpu.SMEM), pl.BlockSpec((LANE_TILE, depth), lambda t: (t, 0))],
        out_specs=pl.BlockSpec((depth, LANE_TILE), lambda t: (0, t)),
        compiler_params=params(),
        cost_estimate=cost(4),
    )(live, values)


def product_kernel(direct, sizes, places, n_arrays, table, *refs):
    arrays, (a_own, a_other, *outs, acc, steps, heads) = refs[:n_arrays], refs[n_arrays:]
    heads[...] = jnp.zeros_like(heads)
    blocks = [n for n in sizes for _ in range(2)]
    runs = []
    for to in range(16 if direct else 4):
        row, base = to * sum(sizes) if direct else 0, 0
        for part, n in enumerate(sizes):
            for q in range(1 if direct else 4):
                at = table[part * 16 + to] if direct else table[part * 16 + to * 4 + q]
                runs.append((0 if direct else to, row, n, pl.ds(pl.multiple_of(base + at * n, 16), n)))
                row += n
            base += 16 * n

    def one_tile(tile, carry):
        lanes = pl.ds(pl.multiple_of(tile * LANE_TILE, LANE_TILE), LANE_TILE)
        base = 0
        for n, ((i, own), (k, other)) in zip(blocks, places, strict=True):
            acc[pl.ds(base, 8 * n), :] = jnp.dot(
                arrays[i][pl.ds(own, 8 * n), :], a_own[:, lanes], preferred_element_type=jnp.float32
            ) + jnp.dot(arrays[k][pl.ds(other, 8 * n), :], a_other[:, lanes], preferred_element_type=jnp.float32)
            base += 8 * n

        encode(acc, steps, heads, tile)
        for to, row, n, source in runs:
            if to == 0 and not direct:
                outs[0][pl.ds(row, n), lanes] = acc[source, :]
            else:
                outs[to][pl.ds(row, n), lanes] = steps[source, :]
        return carry

    lax.fori_loop(0, a_own.shape[1] // LANE_TILE, one_tile, 0)
    for to, row, n, source in runs:
        if direct or to > 0:
            outs[to][pl.ds(row, n), pl.ds(a_own.shape[1], LANES)] = heads[source, :].astype(jnp.int16)


def products(direct, sizes, table, operands, a_own, a_other):
    rows, total = a_own.shape[1], sum(sizes)
    if direct:
        out_shape = [jax.ShapeDtypeStruct((16 * total, rows + LANES), jnp.int16)]
    else:
        out_shape = [jax.ShapeDtypeStruct((4 * total, rows), jnp.float32)] + [
            jax.ShapeDtypeStruct((4 * total, rows + LANES), jnp.int16)
        ] * 3
    arrays = []
    for array, _ in operands:
        if not any(array is known for known in arrays):
            arrays.append(array)
    where = [(next(i for i, known in enumerate(arrays) if known is array), row) for array, row in operands]
    vmem = pl.BlockSpec(memory_space=pltpu.VMEM)
    return pl.pallas_call(
        functools.partial(product_kernel, direct, sizes, list(zip(where[::2], where[1::2])), len(arrays)),
        out_shape=out_shape,
        in_specs=[pl.BlockSpec(memory_space=pltpu.SMEM)] + [vmem] * (len(arrays) + 2),
        out_specs=[vmem] * len(out_shape),
        scratch_shapes=[
            pltpu.VMEM((16 * total, LANE_TILE), jnp.float32),
            pltpu.VMEM((16 * total, LANE_TILE), jnp.int16),
            pltpu.VMEM((16 * total, LANES), jnp.int32),
        ],
        compiler_params=params(),
        cost_estimate=cost(1.5 + total / 5),
    )(table, *arrays, a_own, a_other)


def join_kernel(sizes, table, kept, one, two, three, *outs_and_scratch):
    *outs, total, steps, heads = outs_and_scratch
    heads[...] = jnp.zeros_like(heads)
    everything = pl.ds(0, kept.shape[0])
    runs = []
    for to in range(4):
        row = base = 0
        for part, n in enumerate(sizes):
            runs.append((to, row, n, pl.ds(pl.multiple_of(base + table[part * 4 + to] * n, 16), n)))
            row, base = row + n, base + 4 * n
    for tile in range(kept.shape[1] // LANE_TILE):
        lanes = pl.ds(tile * LANE_TILE, LANE_TILE)
        total[...] = kept[:, lanes] + sum(load_codes(ref, everything, tile) for ref in (one, two, three))
        encode(total, steps, heads, tile)
        for to, row, n, source in runs:
            outs[to][pl.ds(row, n), lanes] = steps[source, :] if to else total[source, :]
    for to, row, n, source in runs:
        if to:
            outs[to][pl.ds(row, n), pl.ds(kept.shape[1], LANES)] = heads[source, :].astype(jnp.int16)


def join(sizes, table, kept, arrived):
    rows, total = kept.shape[1], sum(sizes)
    out_shape = [jax.ShapeDtypeStruct((total, rows), jnp.float32)] + [
        jax.ShapeDtypeStruct((total, rows + LANES), jnp.int16)
    ] * 3
    vmem = pl.BlockSpec(memory_space=pltpu.VMEM)
    return pl.pallas_call(
        functools.partial(join_kernel, sizes),
        out_shape=out_shape,
        in_specs=[pl.BlockSpec(memory_space=pltpu.SMEM)] + [vmem] * 4,
        out_specs=[vmem] * 4,
        scratch_shapes=[
            pltpu.VMEM((4 * total, LANE_TILE), jnp.float32),
            pltpu.VMEM((4 * total, LANE_TILE), jnp.int16),
            pltpu.VMEM((4 * total, LANES), jnp.int32),
        ],
        compiler_params=params(),
        cost_estimate=cost(2.3),
    )(table, kept, *arrived)


def last_kernel(kept, one, two, three, out):
    everything = pl.ds(0, kept.shape[0])
    for tile in range(kept.shape[1] // LANE_TILE):
        lanes = pl.ds(tile * LANE_TILE, LANE_TILE)
        out[:, lanes] = kept[:, lanes] + sum(load_codes(ref, everything, tile) for ref in (one, two, three))


def last(kept, arrived):
    vmem = pl.BlockSpec(memory_space=pltpu.VMEM)
    return pl.pallas_call(
        last_kernel,
        out_shape=jax.ShapeDtypeStruct(kept.shape, jnp.float32),
        in_specs=[vmem] * 4,
        out_specs=vmem,
        compiler_params=params(),
        cost_estimate=cost(1),
    )(kept, *arrived)


def sum_kernel(arrived, out):
    n = out.shape[0]
    for tile in range(out.shape[1] // LANE_TILE):
        out[:, pl.ds(tile * LANE_TILE, LANE_TILE)] = sum(
            load_codes(arrived, pl.ds(k * n, n), tile) for k in range(16)
        )


def sum_of(arrived):
    total, rows = arrived.shape[0] // 16, arrived.shape[1] - LANES
    vmem = pl.BlockSpec(memory_space=pltpu.VMEM)
    return pl.pallas_call(
        sum_kernel,
        out_shape=jax.ShapeDtypeStruct((total, rows), jnp.float32),
        in_specs=[vmem],
        out_specs=vmem,
        compiler_params=params(),
        cost_estimate=cost(1),
    )(arrived)


PLANE_GROUPS = [[index_in_plane(y, z, core) for y in range(4) for z in range(4)] for core in range(2)]
CHUNKS = (32, 16, 16)
GROUPS = (
    (True, (("near", 0),)),
    (False, (("near", 1), ("far", 0))),
    (False, (("near", 2), ("far", 1))),
    (True, (("far", 2),)),
)


def per_device(amps, integrals, amp_live, int_live, row_gap, col_gap):
    x, oj, vert = (lax.axis_index(axis).astype(jnp.int32) for axis in AXES)
    core, y, z = oj % 2, (oj // 2) * 2 + vert // 4, vert % 4
    around = jnp.arange(4, dtype=jnp.int32)

    mine, theirs = turned(core, integrals, int_live)
    depth = mine.shape[2]
    starts = [sum(CHUNKS[:j]) for j in range(len(CHUNKS))]
    cut = lambda half, j: half[:, starts[j]:starts[j] + CHUNKS[j]].reshape(-1, depth)
    swapped = shift(theirs, dcore=1)
    own = [[(cut(mine, j), 0), (cut(swapped, j), 0)] for j in range(len(CHUNKS))]
    join_all = lax.optimization_barrier

    def send(forward, j):
        following = [own[j][0][0], own[j][1][0]] if j < len(CHUNKS) else []
        return (
            shift(jnp.concatenate(forward[0] + following), dx=1),
            shift(jnp.concatenate(forward[1] + following), dx=-1),
        )

    left, right, far = [], [], []

    def receive(arrived, j):
        skip = 8 * CHUNKS[j - 1] if j else 0
        if j:
            far.append([(arrived[0], 0), (arrived[1], 0)])
        if j < len(CHUNKS):
            for side, array in zip((left, right), arrived):
                side.append([(array, skip), (array, skip + 8 * CHUNKS[j])])

    def forward(j):
        held = lambda spot: lax.slice_in_dim(spot[0], spot[1], spot[1] + 8 * CHUNKS[j])
        return [held(left[j][0])], [held(right[j][1])]

    first = send(([], []), 0)
    a_own = turned_amps(amps, after(amp_live, mine))
    a_other = shift(a_own, dcore=1)
    *first, a_own, a_other = join_all((*first, a_own, a_other))
    receive(first, 0)

    def y_run(first_block, places):
        pair = jnp.where(places // 2 == (first_block % 4) // 2, 0, 1)
        return pair * 2 + places % 2

    def spread(direct, parts, previous):
        sizes = tuple(CHUNKS[j] for _, j in parts)
        operands, tables, later = [], [], []
        for kind, j in parts:
            first = x - 1 if kind == "near" else x
            operands += left[j] + right[j] if kind == "near" else own[j] + far[j]
            if direct:
                tables.append((y_run(first, around)[:, None] * 4 + around[None, :]).reshape(16))
            else:
                z_to, y_to = (z + around) % 4, y_run(first, (y + around) % 4)
                z_first = around[None, :] * 4 + z_to[:, None]
                y_first = y_to[:, None] * 4 + around[None, :]
                tables.append(jnp.where(core == 0, z_first, y_first).reshape(16))
                later.append(jnp.where(core == 0, y_to, z_to))
        table = after(jnp.concatenate(tables).astype(jnp.int32), *previous)
        if direct:
            (sent,) = products(True, sizes, table, operands, a_own, a_other)
            got = lax.all_to_all(sent, ("oj", "vert"), 0, 0, axis_index_groups=PLANE_GROUPS, tiled=True)
            return sum_of(got), [sent]
        kept, *sent = products(False, sizes, table, operands, a_own, a_other)
        at_once = sent
        arrived = [shift(s, dplane=((0, d + 1), (d + 1, 0))) for d, s in enumerate(sent)]
        kept, *sent = join(sizes, jnp.concatenate(later).astype(jnp.int32), kept, arrived)
        return last(kept, [shift(s, dplane=((d + 1, 0), (0, d + 1))) for d, s in enumerate(sent)]), at_once

    found, previous = {}, []
    for j, (direct, parts) in enumerate(GROUPS):
        if j < len(CHUNKS):
            coming = send(forward(j), j + 1)
        result, previous = spread(direct, parts, previous)
        if j < len(CHUNKS):
            *coming, previous = join_all((*coming, previous))
            receive(coming, j + 1)
        row = 0
        for kind, j in parts:
            found[kind, j] = result[row:row + CHUNKS[j]]
            row += CHUNKS[j]
    near, far = (jnp.concatenate([found[kind, j] for j in range(len(CHUNKS))]) for kind in ("near", "far"))
    far_is_mine = core == x % 2
    kept = jnp.where(far_is_mine, far, near)
    swapped = shift(jnp.where(far_is_mine, near, far), dcore=1)
    resid = jnp.where(core == 0, jnp.concatenate([kept, swapped]), jnp.concatenate([swapped, kept])).T
    return resid / (row_gap[:, None] + col_gap[None, :])


def solution(mesh):
    return jax.shard_map(
        per_device,
        mesh=mesh,
        in_specs=(
            P("oi", ("oj", "vert")),
            P(("oj", "vert"), "oi"),
            P("oi", ("oj", "vert")),
            P(("oj", "vert"), "oi"),
            P("oi"),
            P(("oj", "vert")),
        ),
        out_specs=P("oi", ("oj", "vert")),
        check_vma=False,
    )
```

```python
import functools
import jax
import jax.numpy as jnp
from jax import lax
from jax.experimental import pallas as pl
from jax.experimental.pallas import tpu as pltpu
from jax.sharding import PartitionSpec as P

AXES = ("oi", "oj", "vert")
SIDE = 4
LANES = 128
LANE_TILE = 512
TOP = 32512.0
STEPS_PER_OCTAVE = 64.0
VMEM_BYTES = 24 * 1024 * 1024


def place_of(i):
    x, rest = divmod(i, 32)
    y_hi, rest = divmod(rest, 16)
    core, rest = divmod(rest, 8)
    y_lo, z = divmod(rest, 4)
    return x, 2 * y_hi + y_lo, z, core


def index_in_plane(y, z, core):
    y, z = y % SIDE, z % SIDE
    return (((y // 2) * 2 + core) * 2 + y % 2) * 4 + z


def shift(value, dx=0, dcore=0, dplane=None):
    pairs = []
    for i in range(128):
        x, y, z, core = place_of(i)
        dy, dz = dplane[core] if dplane else (0, 0)
        pairs.append((i, (x + dx) % SIDE * 32 + index_in_plane(y + dy, z + dz, (core + dcore) % 2)))
    return lax.ppermute(value, AXES, pairs)


def after(value, *others):
    return lax.optimization_barrier((value, others))[0]


def lane_index(rows):
    return lax.broadcasted_iota(jnp.int32, (rows, LANES), 1)


def encode(values, steps, heads, tile):
    for at in range(0, values.shape[0], 32):
        rows = pl.ds(at, min(32, values.shape[0] - at))
        part = values[rows, :]
        peak = jnp.maximum(jnp.max(jnp.abs(part), axis=1, keepdims=True), 1e-30)
        code = jnp.ceil(jnp.log2(peak) * STEPS_PER_OCTAVE)
        scaled = jnp.round(part * (jnp.exp2(code * (-1.0 / STEPS_PER_OCTAVE)) * TOP))
        steps[rows, :] = scaled.astype(jnp.int32).astype(jnp.int16)
        heads[rows, :] = jnp.where(lane_index(rows.size) == tile, code.astype(jnp.int32), heads[rows, :])


def load_codes(ref, rows, tile):
    heads = ref[rows, pl.ds(ref.shape[1] - LANES, LANES)].astype(jnp.int32)
    code = jnp.sum(jnp.where(lane_index(heads.shape[0]) == tile, heads, 0), axis=1, keepdims=True)
    scale = jnp.exp2(code.astype(jnp.float32) * (1.0 / STEPS_PER_OCTAVE)) * (1.0 / TOP)
    return ref[rows, pl.ds(tile * LANE_TILE, LANE_TILE)].astype(jnp.int32).astype(jnp.float32) * scale


def params():
    return pltpu.CompilerParams(vmem_limit_bytes=VMEM_BYTES)


def cost(micros):
    return pl.CostEstimate(flops=int(micros * 1.15e9), bytes_accessed=1000, transcendentals=0)


def turned_kernel(core, live, values, mine, theirs, scratch):
    tile = pl.program_id(0)
    for k in range(values.shape[0] // LANES):
        part = values[pl.ds(k * LANES, LANES), :]
        kept = jnp.where(live[k, tile] != 0, part, jnp.zeros_like(part))
        scratch[:, pl.ds(k * LANES, LANES)] = kept.T
    mine[0] = scratch[pl.ds(pl.multiple_of(core[0] * 64, 16), 64), :]
    theirs[0] = scratch[pl.ds(pl.multiple_of((1 - core[0]) * 64, 16), 64), :]


def turned(core, values, live):
    depth, columns = values.shape
    half = jax.ShapeDtypeStruct((columns // LANES, 64, depth), jnp.bfloat16)
    smem = pl.BlockSpec(memory_space=pltpu.SMEM)
    return pl.pallas_call(
        turned_kernel,
        grid=(columns // LANES,),
        out_shape=[half, half],
        in_specs=[smem, smem, pl.BlockSpec((depth, LANES), lambda t: (0, t))],
        out_specs=[pl.BlockSpec((1, 64, depth), lambda t: (t, 0, 0))] * 2,
        scratch_shapes=[pltpu.VMEM((LANES, depth), jnp.bfloat16)],
        compiler_params=params(),
        cost_estimate=cost(2.5),
    )(core.reshape(1), live, values)


def masked_kernel(live_own, live_other, own, other, out_own, out_other):
    tile = pl.program_id(0)
    for live, values, out in ((live_own, own, out_own), (live_other, other, out_other)):
        for r in range(values.shape[0] // LANES):
            for k in range(values.shape[1] // LANES):
                spot = (pl.ds(r * LANES, LANES), pl.ds(k * LANES, LANES))
                part = values[spot]
                kept = live[tile * (values.shape[0] // LANES) + r, k] != 0
                out[spot] = jnp.where(kept, part, jnp.zeros_like(part))


def masked_amps(live_own, live_other, own, other):
    rows, depth = own.shape
    block = pl.BlockSpec((LANE_TILE, depth), lambda t: (t, 0))
    return pl.pallas_call(
        masked_kernel,
        grid=(rows // LANE_TILE,),
        out_shape=[pltpu.HBM(own.shape, own.dtype)] * 2,
        in_specs=[pl.BlockSpec(memory_space=pltpu.SMEM)] * 2 + [block] * 2,
        out_specs=[block] * 2,
        compiler_params=params(),
        cost_estimate=cost(6),
    )(live_own, live_other, own, other)


def dot_rows(a, b):
    return lax.dot_general(a, b, (((1,), (1,)), ((), ())), preferred_element_type=jnp.float32)


def product_kernel(mode, sizes, places, n_arrays, table, *refs):
    direct = mode == "direct"
    n_outs = 1 if direct else 4
    arrays, halves, refs = refs[:n_arrays], refs[n_arrays:n_arrays + 2], refs[n_arrays + 2:]
    outs, ready, (acc, steps, heads, amps, blocks, in_sems, out_sems) = refs[:n_outs], refs[n_outs:2 * n_outs], refs[2 * n_outs:]
    columns, depth = halves[0].shape
    tiles = columns // LANE_TILE
    kept = None if direct else 0

    def fetch(tile, half):
        return pltpu.make_async_copy(
            halves[half].at[pl.ds(tile * LANE_TILE, LANE_TILE), :], amps.at[tile, half], in_sems.at[tile, half]
        )

    def leave(out, tile):
        lanes = pl.ds(tile * LANE_TILE, LANE_TILE if tile < tiles else LANES)
        return pltpu.make_async_copy(ready[out].at[:, lanes], outs[out].at[:, lanes], out_sems.at[out, tile])

    for half in range(2):
        fetch(0, half).start()
    at = 0
    for n, spots in zip([n for n in sizes for _ in range(2)], places, strict=True):
        for half, (i, first) in enumerate(spots):
            blocks[half, pl.ds(at, 8 * n), :] = arrays[i][pl.ds(first, 8 * n), :]
        at += 8 * n
    heads[...] = jnp.zeros_like(heads)
    runs = []
    for to in range(16 if direct else 4):
        row, base = to * sum(sizes) if direct else 0, 0
        for part, n in enumerate(sizes):
            for q in range(1 if direct else 4):
                at = table[part * 16 + to] if direct else table[part * 16 + to * 4 + q]
                source = pl.ds(pl.multiple_of(base + at * n, 16), n)
                runs.append((0 if direct else to, pl.ds(row, n), source))
                row += n
            base += 16 * n

    for tile in range(tiles):
        lanes = pl.ds(tile * LANE_TILE, LANE_TILE)
        for half in range(2):
            fetch(tile, half).wait()
            if tile + 1 < tiles:
                fetch(tile + 1, half).start()
        acc[...] = dot_rows(blocks[0], amps[tile, 0]) + dot_rows(blocks[1], amps[tile, 1])
        encode(acc, steps, heads, tile)
        for to, into, source in runs:
            ready[to][into, lanes] = acc[source, :] if to == kept else steps[source, :]
        for to in range(n_outs):
            leave(to, tile).start()
    for to, into, source in runs:
        if to != kept:
            ready[to][into, pl.ds(columns, LANES)] = heads[source, :].astype(jnp.int16)
    for to in range(n_outs):
        if to != kept:
            leave(to, tiles).start()
    for to in range(n_outs):
        for tile in range(tiles if to == kept else tiles + 1):
            leave(to, tile).wait()


def products(mode, sizes, table, operands, a_own, a_other):
    (rows, depth), total = a_own.shape, sum(sizes)
    tiles = rows // LANE_TILE
    arrays = []
    for array, _ in operands:
        if not any(array is known for known in arrays):
            arrays.append(array)
    where = [(next(i for i, known in enumerate(arrays) if known is array), row) for array, row in operands]
    if mode == "direct":
        shapes = [((16 * total, rows + LANES), jnp.int16)]
    else:
        shapes = [((4 * total, rows), jnp.float32)] + [((4 * total, rows + LANES), jnp.int16)] * 3
    vmem, hbm = (pl.BlockSpec(memory_space=space) for space in (pltpu.VMEM, pltpu.HBM))
    return pl.pallas_call(
        functools.partial(product_kernel, mode, sizes, list(zip(where[::2], where[1::2])), len(arrays)),
        out_shape=[pltpu.HBM(*shape) for shape in shapes],
        in_specs=[pl.BlockSpec(memory_space=pltpu.SMEM)] + [vmem] * len(arrays) + [hbm] * 2,
        out_specs=[hbm] * len(shapes),
        scratch_shapes=[pltpu.VMEM(*shape) for shape in shapes]
        + [
            pltpu.VMEM((16 * total, LANE_TILE), jnp.float32),
            pltpu.VMEM((16 * total, LANE_TILE), jnp.int16),
            pltpu.VMEM((16 * total, LANES), jnp.int32),
            pltpu.VMEM((tiles, 2, LANE_TILE, depth), jnp.bfloat16),
            pltpu.VMEM((2, 16 * total, depth), jnp.bfloat16),
            pltpu.SemaphoreType.DMA((tiles, 2)),
            pltpu.SemaphoreType.DMA((len(shapes), tiles + 1)),
        ],
        compiler_params=params(),
        cost_estimate=cost(1 + total / 6),
    )(table, *arrays, *(pltpu.with_memory_space_constraint(half, pltpu.HBM) for half in (a_own, a_other)))


def join_kernel(sizes, table, kept, one, two, three, *outs_and_scratch):
    *outs, total, steps, heads = outs_and_scratch
    heads[...] = jnp.zeros_like(heads)
    everything = pl.ds(0, kept.shape[0])
    runs = []
    for to in range(4):
        row = base = 0
        for part, n in enumerate(sizes):
            runs.append((to, row, n, pl.ds(pl.multiple_of(base + table[part * 4 + to] * n, 16), n)))
            row, base = row + n, base + 4 * n
    for tile in range(kept.shape[1] // LANE_TILE):
        lanes = pl.ds(tile * LANE_TILE, LANE_TILE)
        total[...] = kept[:, lanes] + sum(load_codes(ref, everything, tile) for ref in (one, two, three))
        encode(total, steps, heads, tile)
        for to, row, n, source in runs:
            outs[to][pl.ds(row, n), lanes] = steps[source, :] if to else total[source, :]
    for to, row, n, source in runs:
        if to:
            outs[to][pl.ds(row, n), pl.ds(kept.shape[1], LANES)] = heads[source, :].astype(jnp.int16)


def join(sizes, table, kept, arrived):
    rows, total = kept.shape[1], sum(sizes)
    out_shape = [jax.ShapeDtypeStruct((total, rows), jnp.float32)] + [
        jax.ShapeDtypeStruct((total, rows + LANES), jnp.int16)
    ] * 3
    vmem = pl.BlockSpec(memory_space=pltpu.VMEM)
    return pl.pallas_call(
        functools.partial(join_kernel, sizes),
        out_shape=out_shape,
        in_specs=[pl.BlockSpec(memory_space=pltpu.SMEM)] + [vmem] * 4,
        out_specs=[vmem] * 4,
        scratch_shapes=[
            pltpu.VMEM((4 * total, LANE_TILE), jnp.float32),
            pltpu.VMEM((4 * total, LANE_TILE), jnp.int16),
            pltpu.VMEM((4 * total, LANES), jnp.int32),
        ],
        compiler_params=params(),
        cost_estimate=cost(2.3),
    )(table, kept, *arrived)


def last_kernel(kept, one, two, three, out):
    everything = pl.ds(0, kept.shape[0])
    for tile in range(kept.shape[1] // LANE_TILE):
        lanes = pl.ds(tile * LANE_TILE, LANE_TILE)
        out[:, lanes] = kept[:, lanes] + sum(load_codes(ref, everything, tile) for ref in (one, two, three))


def last(kept, arrived):
    vmem = pl.BlockSpec(memory_space=pltpu.VMEM)
    return pl.pallas_call(
        last_kernel,
        out_shape=jax.ShapeDtypeStruct(kept.shape, jnp.float32),
        in_specs=[vmem] * 4,
        out_specs=vmem,
        compiler_params=params(),
        cost_estimate=cost(1),
    )(kept, *arrived)


def sum_kernel(arrived, out):
    n = out.shape[0]
    for tile in range(out.shape[1] // LANE_TILE):
        out[:, pl.ds(tile * LANE_TILE, LANE_TILE)] = sum(
            load_codes(arrived, pl.ds(k * n, n), tile) for k in range(16)
        )


def sum_of(arrived):
    total, rows = arrived.shape[0] // 16, arrived.shape[1] - LANES
    vmem = pl.BlockSpec(memory_space=pltpu.VMEM)
    return pl.pallas_call(
        sum_kernel,
        out_shape=jax.ShapeDtypeStruct((total, rows), jnp.float32),
        in_specs=[vmem],
        out_specs=vmem,
        compiler_params=params(),
        cost_estimate=cost(1),
    )(arrived)


PLANE_GROUPS = [[index_in_plane(y, z, core) for y in range(4) for z in range(4)] for core in range(2)]
CHUNKS = (32, 16, 16)
GROUPS = (
    ("direct", (("near", 0),)),
    ("steps", (("near", 1), ("far", 0))),
    ("steps", (("near", 2), ("far", 1))),
    ("direct", (("far", 2),)),
)


def per_device(amps, integrals, amp_live, int_live, row_gap, col_gap):
    x, oj, vert = (lax.axis_index(axis).astype(jnp.int32) for axis in AXES)
    core, y, z = oj % 2, (oj // 2) * 2 + vert // 4, vert % 4
    around = jnp.arange(4, dtype=jnp.int32)

    mine, theirs = turned(core, integrals, int_live)
    depth = mine.shape[2]
    starts = [sum(CHUNKS[:j]) for j in range(len(CHUNKS))]
    cut = lambda half, j: half[:, starts[j]:starts[j] + CHUNKS[j]].reshape(-1, depth)
    swapped = shift(theirs, dcore=1)
    own = [[(cut(mine, j), 0), (cut(swapped, j), 0)] for j in range(len(CHUNKS))]
    join_all = lax.optimization_barrier

    def send(j):
        held = lambda spot: lax.slice_in_dim(spot[0], spot[1], spot[1] + 8 * CHUNKS[j - 1])
        following = [own[j][0][0], own[j][1][0]] if j < len(CHUNKS) else []
        return (
            shift(jnp.concatenate([held(left[j - 1][0])] + following), dx=1),
            shift(jnp.concatenate([held(right[j - 1][1])] + following), dx=-1),
        )

    left, right, far = [], [], []

    def receive(arrived, j):
        skip = 8 * CHUNKS[j - 1] if j else 0
        if j:
            far.append([(arrived[0], 0), (arrived[1], 0)])
        if j < len(CHUNKS):
            for side, array in zip((left, right), arrived):
                side.append([(array, skip), (array, skip + 8 * CHUNKS[j])])

    own[0] = [(after(own[0][0][0], own[0][1][0]), 0), own[0][1]]
    start = jnp.concatenate([own[0][0][0], own[0][1][0]])
    first = shift(start, dx=1), shift(start, dx=-1)
    live_other, amps_other = shift(amp_live, dcore=1), shift(amps, dcore=1)
    a_both = masked_amps(after(amp_live, start), live_other, amps, amps_other)
    *first, a_both = join_all((*first, a_both))
    receive(first, 0)

    def y_run(first_block, places):
        pair = jnp.where(places // 2 == (first_block % 4) // 2, 0, 1)
        return pair * 2 + places % 2

    def spread(mode, parts, previous):
        sizes = tuple(CHUNKS[j] for _, j in parts)
        operands, tables, later = [], [], []
        for kind, j in parts:
            first = x - 1 if kind == "near" else x
            operands += left[j] + right[j] if kind == "near" else own[j] + far[j]
            if mode == "direct":
                tables.append((y_run(first, around)[:, None] * 4 + around[None, :]).reshape(16))
            else:
                z_to, y_to = (z + around) % 4, y_run(first, (y + around) % 4)
                z_first = around[None, :] * 4 + z_to[:, None]
                y_first = y_to[:, None] * 4 + around[None, :]
                tables.append(jnp.where(core == 0, z_first, y_first).reshape(16))
                later.append(jnp.where(core == 0, y_to, z_to))
        table = after(jnp.concatenate(tables).astype(jnp.int32), *previous)
        if mode == "direct":
            (sent,) = products(mode, sizes, table, operands, *a_both)
            got = lax.all_to_all(sent, ("oj", "vert"), 0, 0, axis_index_groups=PLANE_GROUPS, tiled=True)
            return sum_of(got), [sent]
        kept, *sent = products(mode, sizes, table, operands, *a_both)
        at_once = sent
        arrived = [shift(s, dplane=((0, d + 1), (d + 1, 0))) for d, s in enumerate(sent)]
        kept, *sent = join(sizes, jnp.concatenate(later).astype(jnp.int32), kept, arrived)
        return last(kept, [shift(s, dplane=((d + 1, 0), (0, d + 1))) for d, s in enumerate(sent)]), at_once

    found, previous = {}, []
    for j, (mode, parts) in enumerate(GROUPS):
        if j < len(CHUNKS):
            coming = send(j + 1)
        result, previous = spread(mode, parts, previous)
        if j < len(CHUNKS):
            *coming, previous = join_all((*coming, previous))
            receive(coming, j + 1)
        row = 0
        for kind, j in parts:
            found[kind, j] = result[row:row + CHUNKS[j]]
            row += CHUNKS[j]
    near, far = (jnp.concatenate([found[kind, j] for j in range(len(CHUNKS))]) for kind in ("near", "far"))
    far_is_mine = core == x % 2
    kept = jnp.where(far_is_mine, far, near)
    swapped = shift(jnp.where(far_is_mine, near, far), dcore=1)
    resid = jnp.where(core == 0, jnp.concatenate([kept, swapped]), jnp.concatenate([swapped, kept])).T
    return resid / (row_gap[:, None] + col_gap[None, :])


def solution(mesh):
    return jax.shard_map(
        per_device,
        mesh=mesh,
        in_specs=(
            P("oi", ("oj", "vert")),
            P(("oj", "vert"), "oi"),
            P("oi", ("oj", "vert")),
            P(("oj", "vert"), "oi"),
            P("oi"),
            P(("oj", "vert")),
        ),
        out_specs=P("oi", ("oj", "vert")),
        check_vma=False,
    )
```

```python
import functools
import jax
import jax.numpy as jnp
from jax import lax
from jax.experimental import pallas as pl
from jax.experimental.pallas import tpu as pltpu
from jax.sharding import PartitionSpec as P

AXES = ("oi", "oj", "vert")
SIDE = 4
LANES = 128
LANE_TILE = 512
TOP = 32512.0
STEPS_PER_OCTAVE = 64.0
VMEM_BYTES = 24 * 1024 * 1024


def place_of(i):
    x, rest = divmod(i, 32)
    y_hi, rest = divmod(rest, 16)
    core, rest = divmod(rest, 8)
    y_lo, z = divmod(rest, 4)
    return x, 2 * y_hi + y_lo, z, core


def index_in_plane(y, z, core):
    y, z = y % SIDE, z % SIDE
    return (((y // 2) * 2 + core) * 2 + y % 2) * 4 + z


def shift(value, dx=0, dcore=0, dplane=None):
    pairs = []
    for i in range(128):
        x, y, z, core = place_of(i)
        dy, dz = dplane[core] if dplane else (0, 0)
        pairs.append((i, (x + dx) % SIDE * 32 + index_in_plane(y + dy, z + dz, (core + dcore) % 2)))
    return lax.ppermute(value, AXES, pairs)


def after(value, *others):
    return lax.optimization_barrier((value, others))[0]


def lane_index(rows):
    return lax.broadcasted_iota(jnp.int32, (rows, LANES), 1)


def encode(values, steps, heads, tile):
    for at in range(0, values.shape[0], 32):
        rows = pl.ds(at, min(32, values.shape[0] - at))
        part = values[rows, :]
        peak = jnp.maximum(jnp.max(jnp.abs(part), axis=1, keepdims=True), 1e-30)
        code = jnp.ceil(jnp.log2(peak) * STEPS_PER_OCTAVE)
        scaled = jnp.round(part * (jnp.exp2(code * (-1.0 / STEPS_PER_OCTAVE)) * TOP))
        steps[rows, :] = scaled.astype(jnp.int32).astype(jnp.int16)
        heads[rows, :] = jnp.where(lane_index(rows.size) == tile, code.astype(jnp.int32), heads[rows, :])


def load_codes(ref, rows, tile):
    heads = ref[rows, pl.ds(ref.shape[1] - LANES, LANES)].astype(jnp.int32)
    code = jnp.sum(jnp.where(lane_index(heads.shape[0]) == tile, heads, 0), axis=1, keepdims=True)
    scale = jnp.exp2(code.astype(jnp.float32) * (1.0 / STEPS_PER_OCTAVE)) * (1.0 / TOP)
    return ref[rows, pl.ds(tile * LANE_TILE, LANE_TILE)].astype(jnp.int32).astype(jnp.float32) * scale


def params():
    return pltpu.CompilerParams(vmem_limit_bytes=VMEM_BYTES)


def cost(micros):
    return pl.CostEstimate(flops=int(micros * 1.15e9), bytes_accessed=1000, transcendentals=0)


def turned_kernel(core, live, values, mine, theirs, scratch):
    tile = pl.program_id(0)
    for k in range(values.shape[0] // LANES):
        part = values[pl.ds(k * LANES, LANES), :]
        kept = jnp.where(live[k, tile] != 0, part, jnp.zeros_like(part))
        scratch[:, pl.ds(k * LANES, LANES)] = kept.T
    mine[0] = scratch[pl.ds(pl.multiple_of(core[0] * 64, 16), 64), :]
    theirs[0] = scratch[pl.ds(pl.multiple_of((1 - core[0]) * 64, 16), 64), :]


def turned(core, values, live):
    depth, columns = values.shape
    half = jax.ShapeDtypeStruct((columns // LANES, 64, depth), jnp.bfloat16)
    smem = pl.BlockSpec(memory_space=pltpu.SMEM)
    return pl.pallas_call(
        turned_kernel,
        grid=(columns // LANES,),
        out_shape=[half, half],
        in_specs=[smem, smem, pl.BlockSpec((depth, LANES), lambda t: (0, t))],
        out_specs=[pl.BlockSpec((1, 64, depth), lambda t: (t, 0, 0))] * 2,
        scratch_shapes=[pltpu.VMEM((LANES, depth), jnp.bfloat16)],
        compiler_params=params(),
        cost_estimate=cost(2.5),
    )(core.reshape(1), live, values)


def masked_kernel(live_own, live_other, own, other, out_own, out_other):
    tile = pl.program_id(0)
    for live, values, out in ((live_own, own, out_own), (live_other, other, out_other)):
        for r in range(values.shape[0] // LANES):
            for k in range(values.shape[1] // LANES):
                spot = (pl.ds(r * LANES, LANES), pl.ds(k * LANES, LANES))
                part = values[spot]
                kept = live[tile * (values.shape[0] // LANES) + r, k] != 0
                out[spot] = jnp.where(kept, part, jnp.zeros_like(part))


def masked_amps(live_own, live_other, own, other):
    rows, depth = own.shape
    block = pl.BlockSpec((LANE_TILE, depth), lambda t: (t, 0))
    return pl.pallas_call(
        masked_kernel,
        grid=(rows // LANE_TILE,),
        out_shape=[pltpu.HBM(own.shape, own.dtype)] * 2,
        in_specs=[pl.BlockSpec(memory_space=pltpu.SMEM)] * 2 + [block] * 2,
        out_specs=[block] * 2,
        compiler_params=params(),
        cost_estimate=cost(6),
    )(live_own, live_other, own, other)


def dot_rows(a, b):
    return lax.dot_general(a, b, (((1,), (1,)), ((), ())), preferred_element_type=jnp.float32)


def product_kernel(mode, sizes, places, n_arrays, table, *refs):
    direct = mode == "direct"
    n_outs = 1 if direct else 4
    arrays, halves, refs = refs[:n_arrays], refs[n_arrays:n_arrays + 2], refs[n_arrays + 2:]
    outs, ready, (acc, steps, heads, amps, blocks, in_sems, out_sems) = refs[:n_outs], refs[n_outs:2 * n_outs], refs[2 * n_outs:]
    columns, depth = halves[0].shape
    tiles = columns // LANE_TILE
    kept = None if direct else 0

    def fetch(tile, half):
        return pltpu.make_async_copy(
            halves[half].at[pl.ds(tile * LANE_TILE, LANE_TILE), :], amps.at[tile, half], in_sems.at[tile, half]
        )

    def leave(out, tile):
        last = tile == tiles - 1 and out != kept
        lanes = pl.ds(tile * LANE_TILE, LANE_TILE + LANES if last else LANE_TILE)
        return pltpu.make_async_copy(ready[out].at[:, lanes], outs[out].at[:, lanes], out_sems.at[out, tile])

    for half in range(2):
        fetch(0, half).start()
    at = 0
    for n, spots in zip([n for n in sizes for _ in range(2)], places, strict=True):
        for half, (i, first) in enumerate(spots):
            blocks[half, pl.ds(at, 8 * n), :] = arrays[i][pl.ds(first, 8 * n), :]
        at += 8 * n
    heads[...] = jnp.zeros_like(heads)
    runs = []
    for to in range(16 if direct else 4):
        row, base = to * sum(sizes) if direct else 0, 0
        for part, n in enumerate(sizes):
            for q in range(1 if direct else 4):
                at = table[part * 16 + to] if direct else table[part * 16 + to * 4 + q]
                source = pl.ds(pl.multiple_of(base + at * n, 16), n)
                runs.append((0 if direct else to, pl.ds(row, n), source))
                row += n
            base += 16 * n

    for tile in range(tiles):
        lanes = pl.ds(tile * LANE_TILE, LANE_TILE)
        for half in range(2):
            fetch(tile, half).wait()
            if tile + 1 < tiles:
                fetch(tile + 1, half).start()
            if tile == 0 and half == 0:
                acc[...] = dot_rows(blocks[0], amps[0, 0])
        if tile == 0:
            acc[...] += dot_rows(blocks[1], amps[0, 1])
        else:
            acc[...] = dot_rows(blocks[0], amps[tile, 0]) + dot_rows(blocks[1], amps[tile, 1])
        encode(acc, steps, heads, tile)
        for to, into, source in runs:
            ready[to][into, lanes] = acc[source, :] if to == kept else steps[source, :]
            if tile == tiles - 1 and to != kept:
                ready[to][into, pl.ds(columns, LANES)] = heads[source, :].astype(jnp.int16)
        for to in range(n_outs):
            leave(to, tile).start()
    for to in range(n_outs):
        for tile in range(tiles):
            leave(to, tile).wait()


def products(mode, sizes, table, operands, a_own, a_other):
    (rows, depth), total = a_own.shape, sum(sizes)
    tiles = rows // LANE_TILE
    arrays = []
    for array, _ in operands:
        if not any(array is known for known in arrays):
            arrays.append(array)
    where = [(next(i for i, known in enumerate(arrays) if known is array), row) for array, row in operands]
    if mode == "direct":
        shapes = [((16 * total, rows + LANES), jnp.int16)]
    else:
        shapes = [((4 * total, rows), jnp.float32)] + [((4 * total, rows + LANES), jnp.int16)] * 3
    vmem, hbm = (pl.BlockSpec(memory_space=space) for space in (pltpu.VMEM, pltpu.HBM))
    return pl.pallas_call(
        functools.partial(product_kernel, mode, sizes, list(zip(where[::2], where[1::2])), len(arrays)),
        out_shape=[pltpu.HBM(*shape) for shape in shapes],
        in_specs=[pl.BlockSpec(memory_space=pltpu.SMEM)] + [vmem] * len(arrays) + [hbm] * 2,
        out_specs=[hbm] * len(shapes),
        scratch_shapes=[pltpu.VMEM(*shape) for shape in shapes]
        + [
            pltpu.VMEM((16 * total, LANE_TILE), jnp.float32),
            pltpu.VMEM((16 * total, LANE_TILE), jnp.int16),
            pltpu.VMEM((16 * total, LANES), jnp.int32),
            pltpu.VMEM((tiles, 2, LANE_TILE, depth), jnp.bfloat16),
            pltpu.VMEM((2, 16 * total, depth), jnp.bfloat16),
            pltpu.SemaphoreType.DMA((tiles, 2)),
            pltpu.SemaphoreType.DMA((len(shapes), tiles)),
        ],
        compiler_params=params(),
        cost_estimate=cost(1 + total / 6),
    )(table, *arrays, *(pltpu.with_memory_space_constraint(half, pltpu.HBM) for half in (a_own, a_other)))


def join_kernel(sizes, table, kept, one, two, three, *outs_and_scratch):
    *outs, total, steps, heads = outs_and_scratch
    heads[...] = jnp.zeros_like(heads)
    everything = pl.ds(0, kept.shape[0])
    runs = []
    for to in range(4):
        row = base = 0
        for part, n in enumerate(sizes):
            runs.append((to, row, n, pl.ds(pl.multiple_of(base + table[part * 4 + to] * n, 16), n)))
            row, base = row + n, base + 4 * n
    for tile in range(kept.shape[1] // LANE_TILE):
        lanes = pl.ds(tile * LANE_TILE, LANE_TILE)
        total[...] = kept[:, lanes] + sum(load_codes(ref, everything, tile) for ref in (one, two, three))
        encode(total, steps, heads, tile)
        for to, row, n, source in runs:
            outs[to][pl.ds(row, n), lanes] = steps[source, :] if to else total[source, :]
    for to, row, n, source in runs:
        if to:
            outs[to][pl.ds(row, n), pl.ds(kept.shape[1], LANES)] = heads[source, :].astype(jnp.int16)


def join(sizes, table, kept, arrived):
    rows, total = kept.shape[1], sum(sizes)
    out_shape = [jax.ShapeDtypeStruct((total, rows), jnp.float32)] + [
        jax.ShapeDtypeStruct((total, rows + LANES), jnp.int16)
    ] * 3
    vmem = pl.BlockSpec(memory_space=pltpu.VMEM)
    return pl.pallas_call(
        functools.partial(join_kernel, sizes),
        out_shape=out_shape,
        in_specs=[pl.BlockSpec(memory_space=pltpu.SMEM)] + [vmem] * 4,
        out_specs=[vmem] * 4,
        scratch_shapes=[
            pltpu.VMEM((4 * total, LANE_TILE), jnp.float32),
            pltpu.VMEM((4 * total, LANE_TILE), jnp.int16),
            pltpu.VMEM((4 * total, LANES), jnp.int32),
        ],
        compiler_params=params(),
        cost_estimate=cost(2.3),
    )(table, kept, *arrived)


def last_kernel(kept, one, two, three, out):
    everything = pl.ds(0, kept.shape[0])
    for tile in range(kept.shape[1] // LANE_TILE):
        lanes = pl.ds(tile * LANE_TILE, LANE_TILE)
        out[:, lanes] = kept[:, lanes] + sum(load_codes(ref, everything, tile) for ref in (one, two, three))


def last(kept, arrived):
    vmem = pl.BlockSpec(memory_space=pltpu.VMEM)
    return pl.pallas_call(
        last_kernel,
        out_shape=jax.ShapeDtypeStruct(kept.shape, jnp.float32),
        in_specs=[vmem] * 4,
        out_specs=vmem,
        compiler_params=params(),
        cost_estimate=cost(1),
    )(kept, *arrived)


def sum_kernel(arrived, out):
    n = out.shape[0]
    for tile in range(out.shape[1] // LANE_TILE):
        out[:, pl.ds(tile * LANE_TILE, LANE_TILE)] = sum(
            load_codes(arrived, pl.ds(k * n, n), tile) for k in range(16)
        )


def sum_of(arrived):
    total, rows = arrived.shape[0] // 16, arrived.shape[1] - LANES
    vmem = pl.BlockSpec(memory_space=pltpu.VMEM)
    return pl.pallas_call(
        sum_kernel,
        out_shape=jax.ShapeDtypeStruct((total, rows), jnp.float32),
        in_specs=[vmem],
        out_specs=vmem,
        compiler_params=params(),
        cost_estimate=cost(1),
    )(arrived)


PLANE_GROUPS = [[index_in_plane(y, z, core) for y in range(4) for z in range(4)] for core in range(2)]
CHUNKS = (32, 16, 16)
GROUPS = (
    ("direct", (("near", 0),)),
    ("steps", (("near", 1), ("far", 0))),
    ("steps", (("near", 2), ("far", 1))),
    ("direct", (("far", 2),)),
)


def per_device(amps, integrals, amp_live, int_live, row_gap, col_gap):
    x, oj, vert = (lax.axis_index(axis).astype(jnp.int32) for axis in AXES)
    core, y, z = oj % 2, (oj // 2) * 2 + vert // 4, vert % 4
    around = jnp.arange(4, dtype=jnp.int32)

    mine, theirs = turned(core, integrals, int_live)
    depth = mine.shape[2]
    starts = [sum(CHUNKS[:j]) for j in range(len(CHUNKS))]
    cut = lambda half, j: half[:, starts[j]:starts[j] + CHUNKS[j]].reshape(-1, depth)
    swapped = shift(theirs, dcore=1)
    stacked = [jnp.concatenate([cut(mine, j), cut(swapped, j)]) for j in range(len(CHUNKS))]
    own = [[(stacked[j], 0), (stacked[j], 8 * CHUNKS[j])] for j in range(len(CHUNKS))]
    join_all = lax.optimization_barrier

    def send(j):
        held = lambda spot: lax.slice_in_dim(spot[0], spot[1], spot[1] + 8 * CHUNKS[j - 1])
        following = [stacked[j]] if j < len(CHUNKS) else []
        return (
            shift(jnp.concatenate([held(left[j - 1][0])] + following), dx=1),
            shift(jnp.concatenate([held(right[j - 1][1])] + following), dx=-1),
        )

    left, right, far = [], [], []

    def receive(arrived, j):
        skip = 8 * CHUNKS[j - 1] if j else 0
        if j:
            far.append([(arrived[0], 0), (arrived[1], 0)])
        if j < len(CHUNKS):
            for side, array in zip((left, right), arrived):
                side.append([(array, skip), (array, skip + 8 * CHUNKS[j])])

    start = stacked[0]
    first = shift(start, dx=1), shift(start, dx=-1)
    live_other, amps_other = shift(amp_live, dcore=1), shift(amps, dcore=1)
    a_both = masked_amps(after(amp_live, *stacked), live_other, amps, amps_other)
    *first, a_both = join_all((*first, a_both))
    receive(first, 0)

    def y_run(first_block, places):
        pair = jnp.where(places // 2 == (first_block % 4) // 2, 0, 1)
        return pair * 2 + places % 2

    def spread(mode, parts, previous):
        sizes = tuple(CHUNKS[j] for _, j in parts)
        operands, tables, later = [], [], []
        for kind, j in parts:
            first = x - 1 if kind == "near" else x
            operands += left[j] + right[j] if kind == "near" else own[j] + far[j]
            if mode == "direct":
                tables.append((y_run(first, around)[:, None] * 4 + around[None, :]).reshape(16))
            else:
                z_to, y_to = (z + around) % 4, y_run(first, (y + around) % 4)
                z_first = around[None, :] * 4 + z_to[:, None]
                y_first = y_to[:, None] * 4 + around[None, :]
                tables.append(jnp.where(core == 0, z_first, y_first).reshape(16))
                later.append(jnp.where(core == 0, y_to, z_to))
        table = after(jnp.concatenate(tables).astype(jnp.int32), *previous)
        if mode == "direct":
            (sent,) = products(mode, sizes, table, operands, *a_both)
            got = lax.all_to_all(sent, ("oj", "vert"), 0, 0, axis_index_groups=PLANE_GROUPS, tiled=True)
            return sum_of(got), [sent]
        kept, *sent = products(mode, sizes, table, operands, *a_both)
        at_once = sent
        arrived = [shift(s, dplane=((0, d + 1), (d + 1, 0))) for d, s in enumerate(sent)]
        kept, *sent = join(sizes, jnp.concatenate(later).astype(jnp.int32), kept, arrived)
        return last(kept, [shift(s, dplane=((d + 1, 0), (0, d + 1))) for d, s in enumerate(sent)]), at_once

    found, previous = {}, []
    for j, (mode, parts) in enumerate(GROUPS):
        if j < len(CHUNKS):
            coming = send(j + 1)
        result, previous = spread(mode, parts, previous)
        if j < len(CHUNKS):
            *coming, previous = join_all((*coming, previous))
            receive(coming, j + 1)
        row = 0
        for kind, j in parts:
            found[kind, j] = result[row:row + CHUNKS[j]]
            row += CHUNKS[j]
    near, far = (jnp.concatenate([found[kind, j] for j in range(len(CHUNKS))]) for kind in ("near", "far"))
    far_is_mine = core == x % 2
    kept = jnp.where(far_is_mine, far, near)
    swapped = shift(jnp.where(far_is_mine, near, far), dcore=1)
    resid = jnp.where(core == 0, jnp.concatenate([kept, swapped]), jnp.concatenate([swapped, kept])).T
    return resid / (row_gap[:, None] + col_gap[None, :])


def solution(mesh):
    return jax.shard_map(
        per_device,
        mesh=mesh,
        in_specs=(
            P("oi", ("oj", "vert")),
            P(("oj", "vert"), "oi"),
            P("oi", ("oj", "vert")),
            P(("oj", "vert"), "oi"),
            P("oi"),
            P(("oj", "vert")),
        ),
        out_specs=P("oi", ("oj", "vert")),
        check_vma=False,
    )
```
